512 devices in a mesh: ctx: 64 (over z_hi, x, y), tp: 8 (over z_lo, core).
Axes of the slice: x: 4, y: 4, z: 16 (z_hi: 4, z_lo: 4; z = z_hi * 4 + z_lo), core: 2. Of those that a mesh axis runs over, the one named last changes fastest.
Arguments:
- q_nope: bfloat16 [4096, 8192], P('ctx', 'tp'), may hold values from -4 to 4
- q_rope: bfloat16 [4096, 4096], P('ctx', 'tp'), may hold values from -4 to 4
- kv_cache: bfloat16 [4096, 576], P('ctx'), may hold values from -4 to 4
- w_uk: bfloat16 [64, 128, 512], P('tp'), may hold values from -0.5 to 0.5
- w_uv: bfloat16 [64, 512, 128], P('tp'), may hold values from -0.25 to 0.25
- w_out: bfloat16 [8192, 3584], P('tp', 'ctx'), may hold values from -1 to 1
- group_order: int32 [128], replicated, may hold values from 0 to 127, each once
- block_mask: int32 [128, 128], replicated, may hold values from 0 to 1, as said below
Outputs:
- mixed: bfloat16 [4096, 3584], P('ctx', 'tp')
The draws below stay inside these ranges and needn't reach their ends.
Inputs may be any that keep to these rules, and one draw needn't show every extreme that they name: `group_order`: a permutation of 0 to 127. block_mask[i, i] is 1 and block_mask[i, j] is 0 for j > i.
All inputs are finite; a program needn't handle non-finite values.
Results may differ from the reference program's by a relative error of at most 0.019.
Values may be sent and summed in bfloat16 or wider, within the bound.
A program may use at most 64 MiB of HBM per device.

```python
import jax
import jax.numpy as jnp
from jax import lax

HEADS = 64
NOPE = 128
ROPE = 64
LATENT = 512
VDIM = 128
DO = 3584
LENGTH = 4096
GROUPS = 128
GROUP_LEN = 32


def draw_block_mask(key, part):
    key = jax.random.fold_in(key, 11)
    coin_flips = jax.random.randint(key, (GROUPS, GROUPS), 0, 4)
    row_ids = jnp.arange(GROUPS, dtype=jnp.int32)[:, None]
    col_ids = jnp.arange(GROUPS, dtype=jnp.int32)[None, :]
    below = (col_ids < row_ids) & (coin_flips > 0)
    return jnp.where((col_ids == row_ids) | below, 1, 0).astype(jnp.int32)


def block_levels(own_key, extent, split, least, high):
    level, own = 1.0, jax.random.fold_in(own_key, 6)
    for dim, blocks in split:
        heights = jnp.exp(jax.random.uniform(jax.random.fold_in(own, dim), (blocks,), jnp.float32, least / len(split), high / len(split)))
        level = level * jnp.repeat(heights, extent[dim] // blocks).reshape([-1 if axis == dim else 1 for axis in range(len(extent))])
    return level


def bell_draw(key, dims, scale, reach, shards=(), kind=jnp.bfloat16):
    factor_of = block_levels(key, dims, shards, -0.22, 0.18) if shards else 1.0
    entries = jax.random.normal(key, dims, jnp.float32) * scale * factor_of
    return jnp.minimum(jnp.maximum(entries, -reach), reach).astype(kind)


def setup_inputs(seed: int = 0) -> dict:
    keys = jax.random.split(jax.random.key(seed), 9)
    return {
        "q_nope": bell_draw(keys[0], (LENGTH, HEADS * NOPE), 1.0, 4.0, ((0, 64), (1, 8))),
        "q_rope": bell_draw(keys[1], (LENGTH, HEADS * ROPE), 1.0, 4.0, ((0, 64), (1, 8))),
        "kv_cache": bell_draw(keys[2], (LENGTH, LATENT + ROPE), 1.0, 4.0, ((0, 64),)),
        "w_uk": bell_draw(keys[3], (HEADS, NOPE, LATENT), NOPE ** -0.5, 0.5, ((0, 8),)),
        "w_uv": bell_draw(keys[4], (HEADS, LATENT, VDIM), LATENT ** -0.5, 0.25, ((0, 8),)),
        "w_out": bell_draw(keys[5], (HEADS * VDIM, DO), (HEADS // 2) ** -0.5, 1.0, ((0, 8), (1, 64))),
        "group_order": jax.random.permutation(keys[6], GROUPS).astype(jnp.int32),
        "block_mask": draw_block_mask(jax.random.fold_in(keys[8], 71), 0),
    }


def reference(q_nope, q_rope, kv_cache, w_uk, w_uv, w_out, group_order, block_mask):
    row_ids = jnp.arange(LENGTH, dtype=jnp.int32)
    seq_group = group_order[row_ids // GROUP_LEN]
    positions = seq_group * GROUP_LEN + row_ids % GROUP_LEN
    allowed = (block_mask[seq_group][:, seq_group] == 1) & (positions[None, :] <= positions[:, None])
    score_scale = (NOPE + ROPE) ** -0.5
    nope_heads = q_nope.reshape(LENGTH, HEADS, NOPE)
    rope_heads = q_rope.reshape(LENGTH, HEADS, ROPE)
    latent_keys = kv_cache[:, :LATENT]

    def one_head(head_index):
        absorbed = jnp.dot(nope_heads[:, head_index], w_uk[head_index], preferred_element_type=jnp.float32).astype(jnp.bfloat16)
        queries = jnp.concatenate([absorbed, rope_heads[:, head_index]], axis=1)
        scores = jnp.dot(queries, kv_cache.T, preferred_element_type=jnp.float32) * score_scale
        weights = jnp.where(allowed, jnp.exp(scores), 0.0)
        totals = jnp.sum(weights, axis=1)
        weighted = jnp.dot(weights.astype(jnp.bfloat16), latent_keys, preferred_element_type=jnp.float32)
        latent_out = (weighted / totals[:, None]).astype(jnp.bfloat16)
        return jnp.dot(latent_out, w_uv[head_index], preferred_element_type=jnp.float32).astype(jnp.bfloat16)

    per_head = lax.map(one_head, jnp.arange(HEADS, dtype=jnp.int32))
    head_out = jnp.transpose(per_head, (1, 0, 2)).reshape(LENGTH, HEADS * VDIM)
    return jnp.dot(head_out, w_out, preferred_element_type=jnp.float32).astype(jnp.bfloat16)
```

```python
import jax
import jax.numpy as jnp
from jax import lax
from jax.experimental import pallas as pl
from jax.experimental.pallas import tpu as pltpu
from jax.sharding import PartitionSpec as P

MESH = pl.DeviceIdType.MESH
NT = (((1,), (1,)), ((), ()))
NN = (((1,), (0,)), ((), ()))
F32, BF16, I32 = jnp.float32, jnp.bfloat16, jnp.int32
MASKED = -1e30
N_SEMS = 128


def dot(a, b, dims=NN):
    return lax.dot_general(a, b, dims, preferred_element_type=F32)


def kernel(q_nope, q_rope, kv, w_uk_hbm, w_uv_hbm, w_out, order, mask, out,
           K, W, Q, acc, lanes, bias, w_uk, w_uv, H, XS, XR, S, R, A, send, recv, local):
    heads, nope, latent = w_uk.shape
    rope = q_rope.shape[1] // heads
    half = q_nope.shape[0] // 2
    rows = heads * half
    cols = w_out.shape[1]
    keys = 8 * half
    scale = (nope + rope) ** -0.5 * 1.4426950408889634

    c, t = lax.axis_index("ctx"), lax.axis_index("tp")
    z, x, y = c // 16, (c // 4) % 4, c % 4
    zl, core = t // 2, t % 2
    other = 1 - core

    def dev(dz=0, dx=0, dy=0, dl=0, k=core):
        cc = ((z + dz) % 4) * 16 + ((x + dx) % 4) * 4 + (y + dy) % 4
        return (cc, ((zl + dl) % 4) * 2 + k)

    sibling = dev(k=other)
    pending, used = [], [0]

    def push(src, dst, to):
        i = used[0]
        used[0] += 1
        d = pltpu.make_async_remote_copy(src, dst, send.at[i], recv.at[i], device_id=to, device_id_type=MESH)
        d.start()
        pending.append(d)
        return d

    loads = [pltpu.make_async_copy(w_uk_hbm, w_uk, local.at[0]), pltpu.make_async_copy(w_uv_hbm, w_uv, local.at[1])]
    for d in loads:
        d.start()

    K[0, 0, pl.ds(core, 1), 0] = kv[pl.ds(pl.multiple_of(core * half, half), half), :][None]

    barrier = pltpu.get_barrier_semaphore()
    partners = [dev(dz=1), dev(dz=3), dev(dx=1), dev(dx=3), sibling]
    partners += [dev(dl=dl, dy=dy) for dl in range(4) for dy in range(4) if dl or dy]
    for p in partners:
        pl.semaphore_signal(barrier, inc=1, device_id=p, device_id_type=MESH)
    pl.semaphore_wait(barrier, len(partners))

    lo, hi = pl.ds(0, half // 2), pl.ds(half // 2, half // 2)

    def kz_send():
        a = K.at[0, 0, core, 0]
        return push(a, K.at[3, 0, core, 0], dev(dz=1)), push(a, K.at[1, 0, core, 0], dev(dz=3))

    def kz_relay():
        return (push(K.at[3, 0, core, 0, lo], K.at[2, 0, core, 0, lo], dev(dz=1)),
                push(K.at[1, 0, core, 0, hi], K.at[2, 0, core, 0, hi], dev(dz=3)))

    def kx_send(dz):
        a = K.at[dz, 0, core, 0]
        return push(a, K.at[dz, 0, core, 3], dev(dx=1)), push(a, K.at[dz, 0, core, 1], dev(dx=3))

    def kx_relay(dz):
        return (push(K.at[dz, 0, core, 3, lo], K.at[dz, 0, core, 2, lo], dev(dx=1)),
                push(K.at[dz, 0, core, 1, hi], K.at[dz, 0, core, 2, hi], dev(dx=3)))

    def ky_send(dz):
        a = K.at[dz, 0, core]
        return push(a, K.at[dz, 3, core], dev(dy=1)), push(a, K.at[dz, 1, core], dev(dy=3))

    def ky_relay(dz):
        l, h = pl.ds(0, 2), pl.ds(2, 2)
        return (push(K.at[dz, 3, core, l], K.at[dz, 2, core, l], dev(dy=1)),
                push(K.at[dz, 1, core, h], K.at[dz, 2, core, h], dev(dy=3)))

    def share(dz, dy):
        return push(K.at[dz, dy, core], K.at[dz, dy, core], sibling)

    def arrived(ds):
        for d in ds:
            d.wait_recv()

    own_w = W.at[z, x]
    wl, wh = pl.ds(0, 32), pl.ds(32, 32)

    def wz_send():
        return push(own_w, own_w, dev(dz=1)), push(own_w, own_w, dev(dz=3))

    def wz_relay():
        a, b = W.at[(z + 3) % 4, x, wl], W.at[(z + 1) % 4, x, wh]
        return push(a, a, dev(dz=1)), push(b, b, dev(dz=3))

    def wx_send(dz):
        a = W.at[(z + dz) % 4, x]
        return push(a, a, dev(dx=1)), push(a, a, dev(dx=3))

    def wx_relay(dz):
        zz = (z + dz) % 4
        a, b = W.at[zz, (x + 3) % 4, wl], W.at[zz, (x + 1) % 4, wh]
        return push(a, a, dev(dx=1)), push(b, b, dev(dx=3))

    def attend(dz, dy, first=False):
        kc = K[dz, dy].reshape(keys, latent + rope)
        at = (dz * 4 + dy) * keys
        for i in range(2):
            r = pl.ds(i * rows, rows)
            s = dot(Q[r, :], kc, NT) * scale + bias[i : i + 1, at : at + keys]
            if first:
                key = lax.broadcasted_iota(I32, (rows, keys), 1) - i * keys // 2
                row = lax.broadcasted_iota(I32, (rows, keys), 0) % half
                s = jnp.where((key >= 0) & (key < half) & (key > row), MASKED, s)
            w = jnp.exp2(s)
            part = w[:, :128]
            for j in range(128, keys, 128):
                part = part + w[:, j : j + 128]
            added = dot(w.astype(BF16), kc[:, :latent])
            if first:
                lanes[r, :] = part
                acc[r, :] = added
            else:
                lanes[r, :] += part
                acc[r, :] += added

    kz = kz_send()
    kx = {0: kx_send(0)}

    eye = (lax.broadcasted_iota(I32, (64, cols), 0) == lax.broadcasted_iota(I32, (64, cols), 1)).astype(BF16)
    W[pl.ds(z, 1), pl.ds(x, 1)] = dot(eye, w_out[...], NT).astype(BF16)[None, None]
    wz = wz_send()

    groups = order.shape[1]
    named = (lax.broadcasted_iota(I32, (groups, groups), 0) == order[...]).astype(BF16)
    mine = (lax.broadcasted_iota(I32, (8, groups), 1) == 2 * c + lax.broadcasted_iota(I32, (8, groups), 0)).astype(BF16)
    named_mine = dot(mine, named, NT).astype(BF16)
    by_name = dot(named_mine, mask[...].astype(BF16)).astype(BF16)
    by_store = dot(by_name, named).astype(BF16)
    for n in range(16):
        g = lax.broadcasted_iota(I32, (1, keys), 1) // half
        kk, dx = g // 4, g % 4
        store = 2 * (((z + n // 4) % 4) * 16 + ((x + dx) % 4) * 4 + (y + n % 4) % 4) + kk
        pick = (lax.broadcasted_iota(I32, (groups, keys), 0) == store).astype(BF16)
        bias[:, n * keys : (n + 1) * keys] = (1.0 - dot(by_store, pick)) * MASKED

    arrived(kx[0])
    kx2 = {0: kx_relay(0)}
    arrived(kz)
    kz2 = kz_relay()
    kx[1], kx[3] = kx_send(1), kx_send(3)

    loads[0].wait()
    for h in range(heads):
        a = dot(q_nope[:, h * nope : (h + 1) * nope], w_uk[h]).astype(BF16)
        b = q_rope[:, h * rope : (h + 1) * rope]
        for i in range(2):
            r = pl.ds(i * rows + h * half, half)
            Q[r, :latent] = a[i * half : (i + 1) * half]
            Q[r, latent:] = b[i * half : (i + 1) * half]

    arrived(kx2[0])
    ky, ky2, sh = {0: ky_send(0)}, {}, {(0, 0): share(0, 0)}
    arrived(kz2)
    kx[2] = kx_send(2)
    for dz in (1, 3):
        arrived(kx[dz])
        kx2[dz] = kx_relay(dz)
    arrived(wz)
    wz2 = wz_relay()
    arrived([sh[0, 0]])
    attend(0, 0, True)
    for dz in (1, 3):
        arrived(kx2[dz])
        ky[dz] = ky_send(dz)
        sh[dz, 0] = share(dz, 0)
    arrived(kx[2])
    kx2[2] = kx_relay(2)
    wx, wx2 = {0: wx_send(0)}, {}
    arrived(ky[0])
    ky2[0] = ky_relay(0)
    sh[0, 1], sh[0, 3] = share(0, 1), share(0, 3)
    arrived([sh[1, 0]])
    attend(1, 0)
    arrived(kx2[2])
    ky[2] = ky_send(2)
    sh[2, 0] = share(2, 0)
    wx[1], wx[3] = wx_send(1), wx_send(3)
    arrived([sh[3, 0]])
    attend(3, 0)
    arrived([sh[0, 1]])
    attend(0, 1)
    arrived(wz2)
    wx[2] = wx_send(2)
    before = 0
    for dz in (1, 3, 2):
        arrived(ky[dz])
        ky2[dz] = ky_relay(dz)
        sh[dz, 1], sh[dz, 3] = share(dz, 1), share(dz, 3)
        arrived(ky2[before])
        sh[before, 2] = share(before, 2)
        arrived([sh[before, 3]])
        attend(before, 3)
        arrived(wx[before])
        wx2[before] = wx_relay(before)
        arrived([sh[before, 2]])
        attend(before, 2)
        arrived([sh[dz, 1]])
        attend(dz, 1)
        if dz == 1:
            arrived([sh[2, 0]])
            attend(2, 0)
        before = dz
    arrived([sh[2, 3]])
    attend(2, 3)
    arrived(ky2[2])
    sh[2, 2] = share(2, 2)
    arrived(wx[2])
    wx2[2] = wx_relay(2)
    arrived([sh[2, 2]])
    attend(2, 2)

    loads[1].wait()
    inv = 1.0 / jnp.sum(lanes[...], axis=1, keepdims=True)
    for h in range(heads):
        u, v = h * half, rows + h * half
        a = jnp.concatenate([acc[u : u + half, :] * inv[u : u + half], acc[v : v + half, :] * inv[v : v + half]], axis=0)
        H[0, :, h * 128 : (h + 1) * 128] = dot(a.astype(BF16), w_uv[h]).astype(BF16)
    hy = push(H.at[0], H.at[3], dev(dy=1)), push(H.at[0], H.at[1], dev(dy=3))
    arrived(hy)
    hy2 = (push(H.at[3, wl], H.at[2, wl], dev(dy=1)), push(H.at[1, wh], H.at[2, wh], dev(dy=3)))
    for dz in range(4):
        arrived(wx2[dz])
    arrived(hy2)

    depth = heads * w_uv.shape[2]
    hs = H[...].reshape(4 * 64, depth)

    def product(k):
        return dot(hs, W[:, pl.ds(2 * k, 2)].reshape(512, depth), NT)

    XS[...] = product(other).astype(BF16)
    xs = push(XS, XR, sibling)
    kept = product(core)
    arrived([xs])
    total = (kept + XR[...].astype(F32)).astype(BF16)
    for zz in range(4):
        for dy in range(4):
            S[zz, dy] = total[dy * 64 : (dy + 1) * 64, zz * 128 : (zz + 1) * 128]
    last = [push(S.at[(zl + dl) % 4, dy], R.at[dl, dy], dev(dl=dl, dy=dy))
            for dl in (2, 3, 1, 0) for dy in (2, 1, 3, 0) if dl or dy]
    R[0, 0] = S[pl.ds(zl, 1), 0][0]
    arrived(last)
    for dy in range(4):
        a = R[0, dy].astype(F32) + R[1, dy].astype(F32) + R[2, dy].astype(F32) + R[3, dy].astype(F32)
        A[pl.ds((y + 4 - dy) % 4, 1)] = a[None]
    out[...] = jnp.concatenate(
        [A[yy][:, q * 64 : q * 64 + cols] for q in range(2) for yy in range(4)], axis=1
    ).astype(out.dtype)
    for d in pending:
        d.wait_send()


def solution(mesh):
    def on_device(q_nope, q_rope, kv, w_uk, w_uv, w_out, order, mask):
        heads, nope, latent = w_uk.shape
        rows, width = kv.shape
        half, cols = rows // 2, w_out.shape[1]
        vdim = w_uv.shape[2]
        groups = order.shape[0]
        in_vmem = pl.BlockSpec(memory_space=pltpu.VMEM)
        in_hbm = pl.BlockSpec(memory_space=pl.ANY)
        return pl.pallas_call(
            kernel,
            out_shape=jax.ShapeDtypeStruct((rows, 8 * cols), BF16),
            in_specs=[in_vmem, in_vmem, in_vmem, in_hbm, in_hbm, in_vmem, in_vmem, in_vmem],
            out_specs=in_vmem,
            scratch_shapes=[
                pltpu.VMEM((4, 4, 2, 4, half, width), BF16),
                pltpu.VMEM((4, 4, 64, heads * vdim), BF16),
                pltpu.VMEM((heads * rows, width), BF16),
                pltpu.VMEM((heads * rows, latent), F32),
                pltpu.VMEM((heads * rows, 128), F32),
                pltpu.VMEM((8, 64 * rows), F32),
                pltpu.VMEM(w_uk.shape, BF16),
                pltpu.VMEM(w_uv.shape, BF16),
                pltpu.VMEM((4, rows, heads * vdim), BF16),
                pltpu.VMEM((4 * rows, 512), BF16),
                pltpu.VMEM((4 * rows, 512), BF16),
                pltpu.VMEM((4, 4, rows, 128), BF16),
                pltpu.VMEM((4, 4, rows, 128), BF16),
                pltpu.VMEM((4, rows, 128), F32),
                pltpu.SemaphoreType.DMA((N_SEMS,)),
                pltpu.SemaphoreType.DMA((N_SEMS,)),
                pltpu.SemaphoreType.DMA((2,)),
            ],
            compiler_params=pltpu.CompilerParams(
                collective_id=0, has_side_effects=True, vmem_limit_bytes=48 * 1024 * 1024
            ),
        )(q_nope, q_rope, kv, w_uk, w_uv, w_out, order.reshape(1, groups), mask)

    in_specs = (P("ctx", "tp"), P("ctx", "tp"), P("ctx", None), P("tp", None, None), P("tp", None, None),
                P("tp", "ctx"), P(), P())
    return jax.shard_map(on_device, mesh=mesh, in_specs=in_specs, out_specs=P("ctx", "tp"), check_vma=False)
```

```python
import jax
import jax.numpy as jnp
from jax import lax
from jax.experimental import pallas as pl
from jax.experimental.pallas import tpu as pltpu
from jax.sharding import PartitionSpec as P

MESH = pl.DeviceIdType.MESH
NT = (((1,), (1,)), ((), ()))
NN = (((1,), (0,)), ((), ()))
F32, BF16, I32 = jnp.float32, jnp.bfloat16, jnp.int32
MASKED = -1e30
N_SEMS = 128


def dot(a, b, dims=NN):
    return lax.dot_general(a, b, dims, preferred_element_type=F32)


def kernel(q_nope_hbm, q_rope_hbm, kv_hbm, w_uk_hbm, w_uv_hbm, w_out_hbm, order, mask, out,
           K, W, Q, acc, lanes, bias, q_nope, q_rope, w_uk, w_uv, w_own, H, XS, XR, S, R, A, send, recv, local):
    heads, nope, latent = w_uk.shape
    rope = q_rope.shape[1] // heads
    half = q_nope.shape[0] // 2
    rows = heads * half
    cols = w_own.shape[0]
    keys = 8 * half
    scale = (nope + rope) ** -0.5 * 1.4426950408889634

    c, t = lax.axis_index("ctx"), lax.axis_index("tp")
    z, x, y = c // 16, (c // 4) % 4, c % 4
    zl, core = t // 2, t % 2
    other = 1 - core

    def dev(dz=0, dx=0, dy=0, dl=0, k=core):
        cc = ((z + dz) % 4) * 16 + ((x + dx) % 4) * 4 + (y + dy) % 4
        return (cc, ((zl + dl) % 4) * 2 + k)

    sibling = dev(k=other)
    barrier = pltpu.get_barrier_semaphore()
    partners = [dev(dz=1), dev(dz=3), dev(dx=1), dev(dx=2), dev(dx=3), sibling]
    partners += [dev(dl=dl, dy=dy) for dl in range(4) for dy in range(4) if dl or dy]
    for p in partners:
        pl.semaphore_signal(barrier, inc=1, device_id=p, device_id_type=MESH)

    own_rows = kv_hbm.at[pl.ds(pl.multiple_of(core * half, half), half)]
    loads = [
        pltpu.make_async_copy(src, dst, local.at[i])
        for i, (src, dst) in enumerate([
            (own_rows, K.at[0, 0, core, 0]), (w_out_hbm, w_own), (q_nope_hbm, q_nope), (q_rope_hbm, q_rope),
            (w_uk_hbm, w_uk), (w_uv_hbm, w_uv)])
    ]
    for d in loads:
        d.start()

    pending, used = [], [0]

    def push(src, dst, to):
        i = used[0]
        used[0] += 1
        d = pltpu.make_async_remote_copy(src, dst, send.at[i], recv.at[i], device_id=to, device_id_type=MESH)
        d.start()
        pending.append(d)
        return d

    def arrived(ds):
        for d in ds:
            d.wait_recv()

    lo, hi = pl.ds(0, half // 2), pl.ds(half // 2, half // 2)

    def first(dz, a):
        return dev(dx=a) if dz == 0 else dev(dx=a * other, dy=a * core)

    def second(dz, a):
        return dev(dy=a) if dz == 0 else dev(dx=a * core, dy=a * other)

    def kz_send():
        a = K.at[0, 0, core, 0]
        p, q = K.at[3, 0, core, 0], K.at[1, 0, core, 0]
        l1, h2 = push(a.at[lo], p.at[lo], dev(dz=1)), push(a.at[hi], q.at[hi], dev(dz=3))
        h1, l2 = push(a.at[hi], p.at[hi], dev(dz=1)), push(a.at[lo], q.at[lo], dev(dz=3))
        return l1, h2, h1, l2

    def kz_relay():
        return (push(K.at[3, 0, core, 0, lo], K.at[2, 0, core, 0, lo], dev(dz=1)),
                push(K.at[1, 0, core, 0, hi], K.at[2, 0, core, 0, hi], dev(dz=3)))

    def kf_send(dz):
        return [push(K.at[dz, 0, core, 0], K.at[dz, 0, core, 4 - a], first(dz, a)) for a in (2, 1, 3)]

    def kg_send(dz):
        return {4 - a: push(K.at[dz, 0, core], K.at[dz, 4 - a, core], second(dz, a)) for a in (1, 3, 2)}

    def share(dz, s):
        return push(K.at[dz, s, core], K.at[dz, s, core], sibling)

    own_w = W.at[z, x]
    wl, wh = pl.ds(0, 32), pl.ds(32, 32)

    def wz_send():
        l, h = W.at[z, x, wl], W.at[z, x, wh]
        l1, h2 = push(l, l, dev(dz=1)), push(h, h, dev(dz=3))
        h1, l2 = push(h, h, dev(dz=1)), push(l, l, dev(dz=3))
        return l1, h2, h1, l2

    def wz_relay():
        a, b = W.at[(z + 3) % 4, x, wl], W.at[(z + 1) % 4, x, wh]
        return push(a, a, dev(dz=1)), push(b, b, dev(dz=3))

    def wx_send(dz, part=None, to=(1, 3, 2)):
        a = W.at[(z + dz) % 4, x] if part is None else W.at[(z + dz) % 4, x, part]
        return [push(a, a, dev(dx=d)) for d in to]

    def wx_relay(dz):
        zz = (z + dz) % 4
        a, b = W.at[zz, (x + 3) % 4, wl], W.at[zz, (x + 1) % 4, wh]
        return push(a, a, dev(dx=1)), push(b, b, dev(dx=3))

    def attend(dz, s, begin=False):
        kc = K[dz, s].reshape(keys, latent + rope)
        at = (dz * 4 + s) * keys
        for i in range(2):
            r = pl.ds(i * rows, rows)
            p = dot(Q[r, :], kc, NT) * scale + bias[i : i + 1, at : at + keys]
            if begin:
                key = lax.broadcasted_iota(I32, (rows, keys), 1) - i * keys // 2
                row = lax.broadcasted_iota(I32, (rows, keys), 0) % half
                p = jnp.where((key >= 0) & (key < half) & (key > row), MASKED, p)
            w = jnp.exp2(p)
            part = w[:, :128]
            for j in range(128, keys, 128):
                part = part + w[:, j : j + 128]
            added = dot(w.astype(BF16), kc[:, :latent])
            if begin:
                lanes[r, :] = part
                acc[r, :] = added
            else:
                lanes[r, :] += part
                acc[r, :] += added

    groups = order.shape[1]
    named = (lax.broadcasted_iota(I32, (groups, groups), 0) == order[...]).astype(BF16)
    mine = (lax.broadcasted_iota(I32, (8, groups), 1) == 2 * c + lax.broadcasted_iota(I32, (8, groups), 0)).astype(BF16)
    named_mine = dot(mine, named, NT).astype(BF16)
    by_name = dot(named_mine, mask[...].astype(BF16)).astype(BF16)
    by_store = dot(by_name, named).astype(BF16)
    for n in range(16):
        g = lax.broadcasted_iota(I32, (1, keys), 1) // half
        kk, j = g // 4, g % 4
        dz, s = n // 4, n % 4
        dx, dy = (j, s) if dz == 0 else (jnp.where(kk == 0, j, s), jnp.where(kk == 0, s, j))
        store = 2 * (((z + dz) % 4) * 16 + ((x + dx) % 4) * 4 + (y + dy) % 4) + kk
        pick = (lax.broadcasted_iota(I32, (groups, keys), 0) == store).astype(BF16)
        bias[:, n * keys : (n + 1) * keys] = (1.0 - dot(by_store, pick)) * MASKED

    loads[1].wait()
    own = jnp.concatenate([w_own[...], jnp.zeros((64 - cols, w_own.shape[1]), BF16)], axis=0)
    W[pl.ds(z, 1), pl.ds(x, 1)] = own[None, None]

    for d in loads[2:5]:
        d.wait()
    for h in range(heads):
        a = dot(q_nope[:, h * nope : (h + 1) * nope], w_uk[h]).astype(BF16)
        b = q_rope[:, h * rope : (h + 1) * rope]
        for i in range(2):
            r = pl.ds(i * rows + h * half, half)
            Q[r, :latent] = a[i * half : (i + 1) * half]
            Q[r, latent:] = b[i * half : (i + 1) * half]

    loads[0].wait()
    pl.semaphore_wait(barrier, len(partners))

    kz = kz_send()
    kf, kg, sh = {0: kf_send(0)}, {}, {}
    wx = {0: wx_send(0)}

    def pass_on(dz):
        arrived(kf[dz])
        kg[dz] = kg_send(dz)
        sh[dz, 0] = share(dz, 0)

    def hand_over(dz):
        for s in (3, 1, 2):
            arrived([kg[dz][s]])
            sh[dz, s] = share(dz, s)

    def use(dz, s, begin=False):
        arrived([sh[dz, s]])
        attend(dz, s, begin)

    pass_on(0)
    arrived(kz[:2])
    kz2 = kz_relay()
    arrived(kz[2:])
    kf[1], kf[3] = kf_send(1), kf_send(3)
    wz = wz_send()
    use(0, 0, True)
    pass_on(1)
    pass_on(3)
    arrived(kz2)
    kf[2] = kf_send(2)
    hand_over(0)
    use(0, 3)
    use(0, 1)
    pass_on(2)
    use(0, 2)
    use(1, 0)
    use(3, 0)
    arrived(wz[:2])
    wz2 = wz_relay()
    hand_over(1)
    use(2, 0)
    use(1, 3)
    hand_over(3)
    use(1, 1)
    use(1, 2)
    arrived(wz[2:])
    wx[1], wx[3] = wx_send(1, to=(1, 3)), wx_send(3, to=(1, 3))
    use(3, 3)
    hand_over(2)
    use(3, 1)
    use(3, 2)
    use(2, 3)
    use(2, 1)
    arrived(wx[1])
    arrived(wx[3])
    wx[4], wx[5] = wx_relay(1), wx_relay(3)
    use(2, 2)

    loads[5].wait()
    inv = 1.0 / jnp.sum(lanes[...], axis=1, keepdims=True)
    vdim = w_uv.shape[2]
    piece = heads // 2
    hy = []
    for h in range(heads):
        u, v = h * half, rows + h * half
        a = jnp.concatenate([acc[u : u + half, :] * inv[u : u + half], acc[v : v + half, :] * inv[v : v + half]], axis=0)
        at = (h % piece) * vdim
        H[h // piece, 0, :, at : at + vdim] = dot(a.astype(BF16), w_uv[h]).astype(BF16)
        if h % piece == piece - 1:
            g = h // piece
            hy += [push(H.at[g, 0], H.at[g, 4 - d], dev(dy=d)) for d in (2, 1, 3)]
    arrived(wz2)
    wx[2] = wx_send(2)
    for d in wx:
        if d not in (1, 3):
            arrived(wx[d])
    arrived(hy)

    width = piece * vdim

    def product(k):
        w = W[:, pl.ds(2 * k, 2)].reshape(512, 2 * width)
        a, b = H[0].reshape(256, width), H[1].reshape(256, width)
        return dot(a, w[:, :width], NT) + dot(b, w[:, width:], NT)

    XS[...] = product(other).astype(BF16)
    xs = push(XS, XR, sibling)
    kept = product(core)
    arrived([xs])
    total = (kept + XR[...].astype(F32)).astype(BF16)
    for zz in range(4):
        for dy in range(4):
            S[zz, dy] = total[dy * 64 : (dy + 1) * 64, zz * 128 : (zz + 1) * 128]
    last = [push(S.at[(zl + dl) % 4, dy], R.at[dl, dy], dev(dl=dl, dy=dy))
            for dl in (2, 3, 1, 0) for dy in (2, 1, 3, 0) if dl or dy]
    R[0, 0] = S[pl.ds(zl, 1), 0][0]
    arrived(last)
    for dy in range(4):
        a = R[0, dy].astype(F32) + R[1, dy].astype(F32) + R[2, dy].astype(F32) + R[3, dy].astype(F32)
        A[pl.ds((y + 4 - dy) % 4, 1)] = a[None]
    out[...] = jnp.concatenate(
        [A[yy][:, q * 64 : q * 64 + cols] for q in range(2) for yy in range(4)], axis=1
    ).astype(out.dtype)
    for d in pending:
        d.wait_send()


def solution(mesh):
    def on_device(q_nope, q_rope, kv, w_uk, w_uv, w_out, order, mask):
        heads, nope, latent = w_uk.shape
        rows, width = kv.shape
        half, cols = rows // 2, w_out.shape[1]
        vdim = w_uv.shape[2]
        groups = order.shape[0]
        in_vmem = pl.BlockSpec(memory_space=pltpu.VMEM)
        in_hbm = pl.BlockSpec(memory_space=pl.ANY)
        return pl.pallas_call(
            kernel,
            out_shape=jax.ShapeDtypeStruct((rows, 8 * cols), BF16),
            in_specs=[in_hbm] * 6 + [in_vmem] * 2,
            out_specs=in_vmem,
            scratch_shapes=[
                pltpu.VMEM((4, 4, 2, 4, half, width), BF16),
                pltpu.VMEM((4, 4, 64, heads * vdim), BF16),
                pltpu.VMEM((heads * rows, width), BF16),
                pltpu.VMEM((heads * rows, latent), F32),
                pltpu.VMEM((heads * rows, 128), F32),
                pltpu.VMEM((8, 64 * rows), F32),
                pltpu.VMEM(q_nope.shape, BF16),
                pltpu.VMEM(q_rope.shape, BF16),
                pltpu.VMEM(w_uk.shape, BF16),
                pltpu.VMEM(w_uv.shape, BF16),
                pltpu.VMEM((cols, heads * vdim), BF16),
                pltpu.VMEM((2, 4, rows, heads * vdim // 2), BF16),
                pltpu.VMEM((4 * rows, 512), BF16),
                pltpu.VMEM((4 * rows, 512), BF16),
                pltpu.VMEM((4, 4, rows, 128), BF16),
                pltpu.VMEM((4, 4, rows, 128), BF16),
                pltpu.VMEM((4, rows, 128), F32),
                pltpu.SemaphoreType.DMA((N_SEMS,)),
                pltpu.SemaphoreType.DMA((N_SEMS,)),
                pltpu.SemaphoreType.DMA((6,)),
            ],
            compiler_params=pltpu.CompilerParams(
                collective_id=0, has_side_effects=True, vmem_limit_bytes=60 * 1024 * 1024
            ),
        )(q_nope, q_rope, kv, w_uk, w_uv, w_out.T, order.reshape(1, groups), mask)

    in_specs = (P("ctx", "tp"), P("ctx", "tp"), P("ctx", None), P("tp", None, None), P("tp", None, None),
                P("tp", "ctx"), P(), P())
    return jax.shard_map(on_device, mesh=mesh, in_specs=in_specs, out_specs=P("ctx", "tp"), check_vma=False)
```

```python
import jax
import jax.numpy as jnp
from jax import lax
from jax.experimental import pallas as pl
from jax.experimental.pallas import tpu as pltpu
from jax.sharding import PartitionSpec as P

MESH = pl.DeviceIdType.MESH
NT = (((1,), (1,)), ((), ()))
NN = (((1,), (0,)), ((), ()))
F32, BF16, I32 = jnp.float32, jnp.bfloat16, jnp.int32
MASKED = -1e30
N_SEMS = 128
SWAP = (2,)
RELAY = (0,1,3)


def dot(a, b, dims=NN):
    return lax.dot_general(a, b, dims, preferred_element_type=F32)


def kernel(q_nope_hbm, q_rope_hbm, kv_hbm, w_uk_hbm, w_uv_hbm, w_out_hbm, order, mask, out,
           K, W, Q, acc, lanes, bias, q_nope, q_rope, w_uk, w_uv, w_own, H, XS, XR, S, R, A, send, recv, local):
    heads, nope, latent = w_uk.shape
    rope = q_rope.shape[1] // heads
    half = q_nope.shape[0] // 2
    rows = heads * half
    cols = w_own.shape[0]
    keys = 8 * half
    scale = (nope + rope) ** -0.5 * 1.4426950408889634

    c, t = lax.axis_index("ctx"), lax.axis_index("tp")
    z, x, y = c // 16, (c // 4) % 4, c % 4
    zl, core = t // 2, t % 2
    other = 1 - core

    def dev(dz=0, dx=0, dy=0, dl=0, k=core):
        cc = ((z + dz) % 4) * 16 + ((x + dx) % 4) * 4 + (y + dy) % 4
        return (cc, ((zl + dl) % 4) * 2 + k)

    sibling = dev(k=other)
    barrier = pltpu.get_barrier_semaphore()
    partners = [dev(dz=1), dev(dz=3), dev(dx=1), dev(dx=2), dev(dx=3), sibling]
    partners += [dev(dl=dl, dy=dy) for dl in range(4) for dy in range(4) if dl or dy]
    for p in partners:
        pl.semaphore_signal(barrier, inc=1, device_id=p, device_id_type=MESH)

    own_rows = kv_hbm.at[pl.ds(pl.multiple_of(core * half, half), half)]
    loads = [
        pltpu.make_async_copy(src, dst, local.at[i])
        for i, (src, dst) in enumerate([
            (own_rows, K.at[0, 0, core, 0]), (w_out_hbm, w_own), (q_nope_hbm, q_nope), (q_rope_hbm, q_rope),
            (w_uk_hbm, w_uk), (w_uv_hbm, w_uv)])
    ]
    for d in loads:
        d.start()

    pending, used = [], [0]

    def push(src, dst, to):
        i = used[0]
        used[0] += 1
        d = pltpu.make_async_remote_copy(src, dst, send.at[i], recv.at[i], device_id=to, device_id_type=MESH)
        d.start()
        pending.append(d)
        return d

    done = []

    def sent(d):
        d.wait_send()
        done.append(d)

    def arrived(ds):
        for d in ds:
            d.wait_recv()

    lo, hi = pl.ds(0, half // 2), pl.ds(half // 2, half // 2)

    def first(dz, a):
        return dev(dx=a) if dz not in SWAP else dev(dx=a * other, dy=a * core)

    def second(dz, a):
        return dev(dy=a) if dz not in SWAP else dev(dx=a * core, dy=a * other)

    def kz_send():
        a = K.at[0, 0, core, 0]
        p, q = K.at[3, 0, core, 0], K.at[1, 0, core, 0]
        l1, h2 = push(a.at[lo], p.at[lo], dev(dz=1)), push(a.at[hi], q.at[hi], dev(dz=3))
        h1, l2 = push(a.at[hi], p.at[hi], dev(dz=1)), push(a.at[lo], q.at[lo], dev(dz=3))
        return l1, h2, h1, l2

    def kz_relay():
        return (push(K.at[3, 0, core, 0, lo], K.at[2, 0, core, 0, lo], dev(dz=1)),
                push(K.at[1, 0, core, 0, hi], K.at[2, 0, core, 0, hi], dev(dz=3)))

    def kf_send(dz):
        return [push(K.at[dz, 0, core, 0], K.at[dz, 0, core, 4 - a], first(dz, a)) for a in (2, 1, 3)]

    def kg_send(dz):
        return {4 - a: push(K.at[dz, 0, core], K.at[dz, 4 - a, core], second(dz, a))
                for a in ((1, 3) if dz in RELAY else (1, 3, 2))}

    def kg_relay(dz):
        l, h = pl.ds(0, 2), pl.ds(2, 2)
        return (push(K.at[dz, 3, core, l], K.at[dz, 2, core, l], second(dz, 1)),
                push(K.at[dz, 1, core, h], K.at[dz, 2, core, h], second(dz, 3)))

    def share(dz, s):
        return push(K.at[dz, s, core], K.at[dz, s, core], sibling)

    own_w = W.at[z, x]
    wl, wh = pl.ds(0, 32), pl.ds(32, 32)

    def wz_send(up, down):
        a, b = W.at[z, x, up], W.at[z, x, down]
        return push(a, a, dev(dz=1)), push(b, b, dev(dz=3))

    def wz_relay(at):
        a, b = W.at[(z + 3) % 4, x, pl.ds(at, 16)], W.at[(z + 1) % 4, x, pl.ds(32 + at, 16)]
        return push(a, a, dev(dz=1)), push(b, b, dev(dz=3))

    def wx_send(dz, part, relayed):
        a = W.at[(z + dz) % 4, x, part]
        return [push(a, a, dev(dx=d)) for d in ((1, 3) if relayed else (1, 3, 2))]

    def wx_relay(dz, name):
        d, part = (1, wl) if name == "l" else (3, wh)
        a = W.at[(z + dz) % 4, (x + 4 - d) % 4, part]
        return [push(a, a, dev(dx=d))]

    def attend(dz, s, begin=False):
        kc = K[dz, s].reshape(keys, latent + rope)
        at = (dz * 4 + s) * keys
        for i in range(2):
            r = pl.ds(i * rows, rows)
            p = dot(Q[r, :], kc, NT) * scale + bias[i : i + 1, at : at + keys]
            if begin:
                key = lax.broadcasted_iota(I32, (rows, keys), 1) - i * keys // 2
                row = lax.broadcasted_iota(I32, (rows, keys), 0) % half
                p = jnp.where((key >= 0) & (key < half) & (key > row), MASKED, p)
            w = jnp.exp2(p)
            part = w[:, :128]
            for j in range(128, keys, 128):
                part = part + w[:, j : j + 128]
            added = dot(w.astype(BF16), kc[:, :latent])
            if begin:
                lanes[r, :] = part
                acc[r, :] = added
            else:
                lanes[r, :] += part
                acc[r, :] += added

    groups = order.shape[1]
    named = (lax.broadcasted_iota(I32, (groups, groups), 0) == order[...]).astype(BF16)
    mine = (lax.broadcasted_iota(I32, (8, groups), 1) == 2 * c + lax.broadcasted_iota(I32, (8, groups), 0)).astype(BF16)
    named_mine = dot(mine, named, NT).astype(BF16)
    by_name = dot(named_mine, mask[...].astype(BF16)).astype(BF16)
    by_store = dot(by_name, named).astype(BF16)
    for n in range(16):
        g = lax.broadcasted_iota(I32, (1, keys), 1) // half
        kk, j = g // 4, g % 4
        dz, s = n // 4, n % 4
        dx, dy = (j, s) if dz not in SWAP else (jnp.where(kk == 0, j, s), jnp.where(kk == 0, s, j))
        store = 2 * (((z + dz) % 4) * 16 + ((x + dx) % 4) * 4 + (y + dy) % 4) + kk
        pick = (lax.broadcasted_iota(I32, (groups, keys), 0) == store).astype(BF16)
        bias[:, n * keys : (n + 1) * keys] = (1.0 - dot(by_store, pick)) * MASKED

    loads[1].wait()
    own = jnp.concatenate([w_own[...], jnp.zeros((64 - cols, w_own.shape[1]), BF16)], axis=0)
    W[pl.ds(z, 1), pl.ds(x, 1)] = own[None, None]

    for d in loads[2:5]:
        d.wait()
    for h in range(heads):
        a = dot(q_nope[:, h * nope : (h + 1) * nope], w_uk[h]).astype(BF16)
        b = q_rope[:, h * rope : (h + 1) * rope]
        for i in range(2):
            r = pl.ds(i * rows + h * half, half)
            Q[r, :latent] = a[i * half : (i + 1) * half]
            Q[r, latent:] = b[i * half : (i + 1) * half]

    loads[0].wait()
    pl.semaphore_wait(barrier, len(partners))

    kz = kz_send()
    kf, kg, kg2, sh = {0: kf_send(0)}, {}, {}, {}
    wz = []
    wx, wx2 = {}, {}

    def wx_go(dz, name, relayed=True):
        wx[dz, name] = wx_send(dz, halves[name], relayed)

    def wx_on(dz, name):
        arrived(wx[dz, name])
        wx2[dz, name] = wx_relay(dz, name)

    halves = {"l": wl, "h": wh, "a": pl.ds(0, 16), "b": pl.ds(16, 16), "c": pl.ds(32, 16), "d": pl.ds(48, 16)}
    wx_go(0, "l")
    wx_go(0, "h")

    def pass_on(dz):
        arrived(kf[dz])
        kg[dz] = kg_send(dz)
        sh[dz, 0] = share(dz, 0)

    def hand_over(dz):
        if dz in RELAY:
            arrived([kg[dz][3], kg[dz][1]])
            kg2[dz] = kg_relay(dz)
        for s in (3, 1):
            arrived([] if dz in RELAY else [kg[dz][s]])
            sh[dz, s] = share(dz, s)

    def hand_over_far(dz):
        arrived(kg2[dz] if dz in RELAY else [kg[dz][2]])
        sh[dz, 2] = share(dz, 2)

    def use(dz, s, begin=False):
        arrived([sh[dz, s]])
        attend(dz, s, begin)

    pass_on(0)
    wz.append(wz_send(wl, wh))
    arrived(kz[:2])
    kz2 = kz_relay()
    arrived(kz[2:])
    kf[1], kf[3] = kf_send(1), kf_send(3)
    use(0, 0, True)
    hand_over(0)
    wx_on(0, "l")
    wx_on(0, "h")
    pass_on(1)
    pass_on(3)
    arrived(kz2)
    kf[2] = kf_send(2)
    wz.append(wz_send(wh, wl))
    hand_over_far(0)
    arrived(wz[0])
    wz2 = [wz_relay(0)]
    wx_go(3, "l")
    wx_go(1, "h")
    use(0, 3)
    use(0, 1)
    pass_on(2)
    hand_over(1)
    hand_over(3)
    wz2.append(wz_relay(16))
    use(0, 2)
    arrived(wz[1])
    wx_go(3, "h")
    wx_go(1, "l")
    use(1, 0)
    use(3, 0)
    wx_on(3, "l")
    wx_on(1, "h")
    hand_over_far(1)
    hand_over_far(3)
    use(1, 3)
    use(2, 0)
    use(1, 1)
    hand_over(2)
    arrived(wz2[0])
    wx_go(2, "a", False)
    wx_go(2, "c", False)
    use(3, 3)
    use(3, 1)
    hand_over_far(2)
    use(1, 2)
    wx_on(3, "h")
    wx_on(1, "l")
    use(3, 2)
    use(2, 3)
    arrived(wz2[1])
    wx_go(2, "b", False)
    wx_go(2, "d", False)
    use(2, 1)
    use(2, 2)

    loads[5].wait()
    inv = 1.0 / jnp.sum(lanes[...], axis=1, keepdims=True)
    vdim = w_uv.shape[2]
    piece = heads // 2
    hy = []
    for h in range(heads):
        u, v = h * half, rows + h * half
        a = jnp.concatenate([acc[u : u + half, :] * inv[u : u + half], acc[v : v + half, :] * inv[v : v + half]], axis=0)
        at = (h % piece) * vdim
        H[h // piece, 0, :, at : at + vdim] = dot(a.astype(BF16), w_uv[h]).astype(BF16)
        if h % piece == piece - 1:
            g = h // piece
            hy += [push(H.at[g, 0], H.at[g, 4 - d], dev(dy=d)) for d in (2, 1, 3)]
    for name in "acbd":
        arrived(wx[2, name])
    for d in wx2:
        arrived(wx2[d])
    arrived(hy)

    width = piece * vdim

    def product(k):
        w = W[:, pl.ds(2 * k, 2)].reshape(512, 2 * width)
        a, b = H[0].reshape(256, width), H[1].reshape(256, width)
        return dot(a, w[:, :width], NT) + dot(b, w[:, width:], NT)

    XS[...] = product(other).astype(BF16)
    xs = push(XS, XR, sibling)
    kept = product(core)
    arrived([xs])
    total = (kept + XR[...].astype(F32)).astype(BF16)
    for zz in range(4):
        for dy in range(4):
            S[zz, dy] = total[dy * 64 : (dy + 1) * 64, zz * 128 : (zz + 1) * 128]
    last = [push(S.at[(zl + dl) % 4, dy], R.at[dl, dy], dev(dl=dl, dy=dy))
            for dl in (2, 3, 1, 0) for dy in (2, 1, 3, 0) if dl or dy]
    R[0, 0] = S[pl.ds(zl, 1), 0][0]
    arrived(last)
    for dy in range(4):
        a = R[0, dy].astype(F32) + R[1, dy].astype(F32) + R[2, dy].astype(F32) + R[3, dy].astype(F32)
        A[pl.ds((y + 4 - dy) % 4, 1)] = a[None]
    out[...] = jnp.concatenate(
        [A[yy][:, q * 64 : q * 64 + cols] for q in range(2) for yy in range(4)], axis=1
    ).astype(out.dtype)
    for d in pending:
        if not any(d is e for e in done):
            d.wait_send()


def solution(mesh):
    def on_device(q_nope, q_rope, kv, w_uk, w_uv, w_out, order, mask):
        heads, nope, latent = w_uk.shape
        rows, width = kv.shape
        half, cols = rows // 2, w_out.shape[1]
        vdim = w_uv.shape[2]
        groups = order.shape[0]
        in_vmem = pl.BlockSpec(memory_space=pltpu.VMEM)
        in_hbm = pl.BlockSpec(memory_space=pl.ANY)
        return pl.pallas_call(
            kernel,
            out_shape=jax.ShapeDtypeStruct((rows, 8 * cols), BF16),
            in_specs=[in_hbm] * 6 + [in_vmem] * 2,
            out_specs=in_vmem,
            scratch_shapes=[
                pltpu.VMEM((4, 4, 2, 4, half, width), BF16),
                pltpu.VMEM((4, 4, 64, heads * vdim), BF16),
                pltpu.VMEM((heads * rows, width), BF16),
                pltpu.VMEM((heads * rows, latent), F32),
                pltpu.VMEM((heads * rows, 128), F32),
                pltpu.VMEM((8, 64 * rows), F32),
                pltpu.VMEM(q_nope.shape, BF16),
                pltpu.VMEM(q_rope.shape, BF16),
                pltpu.VMEM(w_uk.shape, BF16),
                pltpu.VMEM(w_uv.shape, BF16),
                pltpu.VMEM((cols, heads * vdim), BF16),
                pltpu.VMEM((2, 4, rows, heads * vdim // 2), BF16),
                pltpu.VMEM((4 * rows, 512), BF16),
                pltpu.VMEM((4 * rows, 512), BF16),
                pltpu.VMEM((4, 4, rows, 128), BF16),
                pltpu.VMEM((4, 4, rows, 128), BF16),
                pltpu.VMEM((4, rows, 128), F32),
                pltpu.SemaphoreType.DMA((N_SEMS,)),
                pltpu.SemaphoreType.DMA((N_SEMS,)),
                pltpu.SemaphoreType.DMA((6,)),
            ],
            compiler_params=pltpu.CompilerParams(
                collective_id=0, has_side_effects=True, vmem_limit_bytes=60 * 1024 * 1024
            ),
        )(q_nope, q_rope, kv, w_uk, w_uv, w_out.T, order.reshape(1, groups), mask)

    in_specs = (P("ctx", "tp"), P("ctx", "tp"), P("ctx", None), P("tp", None, None), P("tp", None, None),
                P("tp", "ctx"), P(), P())
    return jax.shard_map(on_device, mesh=mesh, in_specs=in_specs, out_specs=P("ctx", "tp"), check_vma=False)
```

```python
import jax
import jax.numpy as jnp
from jax import lax
from jax.experimental import pallas as pl
from jax.experimental.pallas import tpu as pltpu
from jax.sharding import PartitionSpec as P

MESH = pl.DeviceIdType.MESH
NT = (((1,), (1,)), ((), ()))
NN = (((1,), (0,)), ((), ()))
F32, BF16, I32 = jnp.float32, jnp.bfloat16, jnp.int32
MASKED = -1e30
N_SEMS = 128
SWAP = (2,)
RELAY = (0,1,3)


def dot(a, b, dims=NN):
    return lax.dot_general(a, b, dims, preferred_element_type=F32)


def kernel(q_nope_hbm, q_rope_hbm, kv_hbm, w_uk_hbm, w_uv_hbm, w_out_hbm, order, mask, out,
           K, W, Q, acc, lanes, bias, q_nope, q_rope, w_uk, w_uv, w_own, H, XS, XR, S, R, A, send, recv, local):
    heads, nope, latent = w_uk.shape
    rope = q_rope.shape[1] // heads
    half = q_nope.shape[0] // 2
    rows = heads * half
    cols = w_own.shape[0]
    keys = 8 * half
    scale = (nope + rope) ** -0.5 * 1.4426950408889634

    c, t = lax.axis_index("ctx"), lax.axis_index("tp")
    z, x, y = c // 16, (c // 4) % 4, c % 4
    zl, core = t // 2, t % 2
    other = 1 - core

    def dev(dz=0, dx=0, dy=0, dl=0, k=core):
        cc = ((z + dz) % 4) * 16 + ((x + dx) % 4) * 4 + (y + dy) % 4
        return (cc, ((zl + dl) % 4) * 2 + k)

    sibling = dev(k=other)
    barrier = pltpu.get_barrier_semaphore()
    partners = [dev(dz=1), dev(dz=3), dev(dx=1), dev(dx=2), dev(dx=3), sibling]
    partners += [dev(dl=dl, dy=dy) for dl in range(4) for dy in range(4) if dl or dy]
    for p in partners:
        pl.semaphore_signal(barrier, inc=1, device_id=p, device_id_type=MESH)

    own_rows = kv_hbm.at[pl.ds(pl.multiple_of(core * half, half), half)]
    loads = [
        pltpu.make_async_copy(src, dst, local.at[i])
        for i, (src, dst) in enumerate([
            (own_rows, K.at[0, 0, core, 0]), (w_out_hbm, w_own), (q_nope_hbm, q_nope), (q_rope_hbm, q_rope),
            (w_uk_hbm, w_uk), (w_uv_hbm, w_uv)])
    ]
    for d in loads:
        d.start()

    pending, used = [], [0]

    def push(src, dst, to):
        i = used[0]
        used[0] += 1
        d = pltpu.make_async_remote_copy(src, dst, send.at[i], recv.at[i], device_id=to, device_id_type=MESH)
        d.start()
        pending.append(d)
        return d

    done = []

    def sent(d):
        d.wait_send()
        done.append(d)

    def arrived(ds):
        for d in ds:
            d.wait_recv()

    lo, hi = pl.ds(0, half // 2), pl.ds(half // 2, half // 2)

    def first(dz, a):
        return dev(dx=a) if dz not in SWAP else dev(dx=a * other, dy=a * core)

    def second(dz, a):
        return dev(dy=a) if dz not in SWAP else dev(dx=a * core, dy=a * other)

    def kz_send():
        a = K.at[0, 0, core, 0]
        p, q = K.at[3, 0, core, 0], K.at[1, 0, core, 0]
        l1, h2 = push(a.at[lo], p.at[lo], dev(dz=1)), push(a.at[hi], q.at[hi], dev(dz=3))
        h1, l2 = push(a.at[hi], p.at[hi], dev(dz=1)), push(a.at[lo], q.at[lo], dev(dz=3))
        return l1, h2, h1, l2

    def kz_relay():
        return (push(K.at[3, 0, core, 0, lo], K.at[2, 0, core, 0, lo], dev(dz=1)),
                push(K.at[1, 0, core, 0, hi], K.at[2, 0, core, 0, hi], dev(dz=3)))

    def kf_send(dz):
        return [push(K.at[dz, 0, core, 0], K.at[dz, 0, core, 4 - a], first(dz, a)) for a in (2, 1, 3)]

    def kg_send(dz):
        return {4 - a: push(K.at[dz, 0, core], K.at[dz, 4 - a, core], second(dz, a))
                for a in ((1, 3) if dz in RELAY else (1, 3, 2))}

    def kg_relay(dz):
        l, h = pl.ds(0, 2), pl.ds(2, 2)
        return (push(K.at[dz, 3, core, l], K.at[dz, 2, core, l], second(dz, 1)),
                push(K.at[dz, 1, core, h], K.at[dz, 2, core, h], second(dz, 3)))

    def share(dz, s):
        return push(K.at[dz, s, core], K.at[dz, s, core], sibling)

    own_w = W.at[z, x]
    wl, wh = pl.ds(0, 32), pl.ds(32, 32)

    def wz_send(up, down):
        a, b = W.at[z, x, up], W.at[z, x, down]
        return push(a, a, dev(dz=1)), push(b, b, dev(dz=3))

    def wz_relay(at):
        a, b = W.at[(z + 3) % 4, x, pl.ds(at, 16)], W.at[(z + 1) % 4, x, pl.ds(32 + at, 16)]
        return push(a, a, dev(dz=1)), push(b, b, dev(dz=3))

    def wx_send(dz, part, relayed):
        a = W.at[(z + dz) % 4, x, part]
        return [push(a, a, dev(dx=d)) for d in ((1, 3) if relayed else (1, 3, 2))]

    def wx_relay(dz, name):
        d, part = (1, wl) if name == "l" else (3, wh)
        a = W.at[(z + dz) % 4, (x + 4 - d) % 4, part]
        return [push(a, a, dev(dx=d))]

    def attend(dz, s, begin=False):
        kc = K[dz, s].reshape(keys, latent + rope)
        at = (dz * 4 + s) * keys
        for i in range(2):
            r = pl.ds(i * rows, rows)
            p = dot(Q[r, :], kc, NT) * scale + bias[i : i + 1, at : at + keys]
            if begin:
                key = lax.broadcasted_iota(I32, (rows, keys), 1) - i * keys // 2
                row = lax.broadcasted_iota(I32, (rows, keys), 0) % half
                p = jnp.where((key >= 0) & (key < half) & (key > row), MASKED, p)
            w = jnp.exp2(p)
            part = w[:, :128]
            for j in range(128, keys, 128):
                part = part + w[:, j : j + 128]
            added = dot(w.astype(BF16), kc[:, :latent])
            if begin:
                lanes[r, :] = part
                acc[r, :] = added
            else:
                lanes[r, :] += part
                acc[r, :] += added

    groups = order.shape[1]
    named = (lax.broadcasted_iota(I32, (groups, groups), 0) == order[...]).astype(BF16)
    mine = (lax.broadcasted_iota(I32, (8, groups), 1) == 2 * c + lax.broadcasted_iota(I32, (8, groups), 0)).astype(BF16)
    named_mine = dot(mine, named, NT).astype(BF16)
    by_name = dot(named_mine, mask[...].astype(BF16)).astype(BF16)
    by_store = dot(by_name, named).astype(BF16)
    for n in range(16):
        g = lax.broadcasted_iota(I32, (1, keys), 1) // half
        kk, j = g // 4, g % 4
        dz, s = n // 4, n % 4
        dx, dy = (j, s) if dz not in SWAP else (jnp.where(kk == 0, j, s), jnp.where(kk == 0, s, j))
        store = 2 * (((z + dz) % 4) * 16 + ((x + dx) % 4) * 4 + (y + dy) % 4) + kk
        pick = (lax.broadcasted_iota(I32, (groups, keys), 0) == store).astype(BF16)
        bias[:, n * keys : (n + 1) * keys] = (1.0 - dot(by_store, pick)) * MASKED

    loads[1].wait()
    own = jnp.concatenate([w_own[...], jnp.zeros((64 - cols, w_own.shape[1]), BF16)], axis=0)
    W[pl.ds(z, 1), pl.ds(x, 1)] = own[None, None]

    for d in loads[2:5]:
        d.wait()
    for h in range(heads):
        a = dot(q_nope[:, h * nope : (h + 1) * nope], w_uk[h]).astype(BF16)
        b = q_rope[:, h * rope : (h + 1) * rope]
        for i in range(2):
            r = pl.ds(i * rows + h * half, half)
            Q[r, :latent] = a[i * half : (i + 1) * half]
            Q[r, latent:] = b[i * half : (i + 1) * half]

    loads[0].wait()
    pl.semaphore_wait(barrier, len(partners))

    kz = kz_send()
    kf, kg, kg2, sh = {0: kf_send(0)}, {}, {}, {}
    wz = []
    wx, wx2 = {}, {}

    def wx_go(dz, name, relayed=True):
        wx[dz, name] = wx_send(dz, halves[name], relayed)

    def wx_on(dz, name):
        arrived(wx[dz, name])
        wx2[dz, name] = wx_relay(dz, name)

    halves = {"l": wl, "h": wh, "a": pl.ds(0, 16), "b": pl.ds(16, 16), "c": pl.ds(32, 16), "d": pl.ds(48, 16)}
    wx_go(0, "l")
    wx_go(0, "h")

    def pass_on(dz):
        arrived(kf[dz])
        kg[dz] = kg_send(dz)
        sh[dz, 0] = share(dz, 0)

    def hand_over(dz):
        if dz in RELAY:
            arrived([kg[dz][3], kg[dz][1]])
            kg2[dz] = kg_relay(dz)
        for s in (3, 1):
            arrived([] if dz in RELAY else [kg[dz][s]])
            sh[dz, s] = share(dz, s)

    def hand_over_far(dz):
        arrived(kg2[dz] if dz in RELAY else [kg[dz][2]])
        sh[dz, 2] = share(dz, 2)

    def use(dz, s, begin=False):
        arrived([sh[dz, s]])
        attend(dz, s, begin)

    pass_on(0)
    wz.append(wz_send(wl, wh))
    arrived(kz[:2])
    kz2 = kz_relay()
    arrived(kz[2:])
    kf[1], kf[3] = kf_send(1), kf_send(3)
    use(0, 0, True)
    hand_over(0)
    wx_on(0, "l")
    wx_on(0, "h")
    pass_on(1)
    pass_on(3)
    arrived(kz2)
    kf[2] = kf_send(2)
    wz.append(wz_send(wh, wl))
    hand_over_far(0)
    arrived(wz[0])
    wz2 = [wz_relay(0)]
    wx_go(3, "l")
    wx_go(1, "h")
    use(0, 3)
    use(0, 1)
    pass_on(2)
    hand_over(1)
    hand_over(3)
    wz2.append(wz_relay(16))
    use(0, 2)
    arrived(wz[1])
    wx_go(3, "h")
    wx_go(1, "l")
    use(1, 0)
    use(3, 0)
    wx_on(3, "l")
    wx_on(1, "h")
    hand_over_far(1)
    hand_over_far(3)
    use(1, 3)
    use(2, 0)
    use(1, 1)
    hand_over(2)
    arrived(wz2[0])
    wx_go(2, "a", False)
    wx_go(2, "c", False)
    use(3, 3)
    use(3, 1)
    hand_over_far(2)
    use(1, 2)
    wx_on(3, "h")
    wx_on(1, "l")
    use(3, 2)
    use(2, 3)
    arrived(wz2[1])
    wx_go(2, "b", False)
    wx_go(2, "d", False)
    use(2, 1)
    use(2, 2)

    loads[5].wait()
    inv = 1.0 / jnp.sum(lanes[...], axis=1, keepdims=True)
    vdim = w_uv.shape[2]
    piece = heads // 2
    hy = []
    for h in range(heads):
        u, v = h * half, rows + h * half
        a = jnp.concatenate([acc[u : u + half, :] * inv[u : u + half], acc[v : v + half, :] * inv[v : v + half]], axis=0)
        at = (h % piece) * vdim
        H[h // piece, 0, :, at : at + vdim] = dot(a.astype(BF16), w_uv[h]).astype(BF16)
        if h % piece == piece - 1:
            g = h // piece
            hy += [push(H.at[g, 0], H.at[g, 4 - d], dev(dy=d)) for d in (1, 3, 2)]
    for name in "acbd":
        arrived(wx[2, name])
    for d in wx2:
        arrived(wx2[d])
    hy = {(i // 3, (3, 1, 2)[i % 3]): d for i, d in enumerate(hy)}
    arrived([hy[g, d] for g in range(2) for d in (1, 3)])

    deep = W.shape[3] // 2

    def product(k, at):
        w = W[:, pl.ds(2 * k, 2)].reshape(512, 2 * deep)
        a, b = (H[g, at : at + 2].reshape(128, deep) for g in range(2))
        return dot(a, w[:, :deep], NT) + dot(b, w[:, deep:], NT)

    last = []
    for at in (0, 2):
        if at:
            arrived([hy[g, 2] for g in range(2)])
        r = pl.ds(at * 64, 128)
        XS[r, :] = product(other, at).astype(BF16)
        xs = push(XS.at[r], XR.at[r], sibling)
        kept = product(core, at)
        arrived([xs])
        total = (kept + XR[r, :].astype(F32)).astype(BF16)
        for zz in range(4):
            for i in range(2):
                S[zz, at + i] = total[i * 64 : (i + 1) * 64, zz * 128 : (zz + 1) * 128]
        last += [push(S.at[(zl + dl) % 4, dy], R.at[dl, dy], dev(dl=dl, dy=dy))
                 for dl in (2, 3, 1, 0) for dy in (at, at + 1) if dl or dy]
    R[0, 0] = S[pl.ds(zl, 1), 0][0]
    arrived(last)
    for dy in range(4):
        a = R[0, dy].astype(F32) + R[1, dy].astype(F32) + R[2, dy].astype(F32) + R[3, dy].astype(F32)
        A[pl.ds((y + 4 - dy) % 4, 1)] = a[None]
    out[...] = jnp.concatenate(
        [A[yy][:, q * 64 : q * 64 + cols] for q in range(2) for yy in range(4)], axis=1
    ).astype(out.dtype)
    for d in pending:
        if not any(d is e for e in done):
            d.wait_send()


def solution(mesh):
    def on_device(q_nope, q_rope, kv, w_uk, w_uv, w_out, order, mask):
        heads, nope, latent = w_uk.shape
        rows, width = kv.shape
        half, cols = rows // 2, w_out.shape[1]
        vdim = w_uv.shape[2]
        groups = order.shape[0]
        in_vmem = pl.BlockSpec(memory_space=pltpu.VMEM)
        in_hbm = pl.BlockSpec(memory_space=pl.ANY)
        return pl.pallas_call(
            kernel,
            out_shape=jax.ShapeDtypeStruct((rows, 8 * cols), BF16),
            in_specs=[in_hbm] * 6 + [in_vmem] * 2,
            out_specs=in_vmem,
            scratch_shapes=[
                pltpu.VMEM((4, 4, 2, 4, half, width), BF16),
                pltpu.VMEM((4, 4, 64, heads * vdim), BF16),
                pltpu.VMEM((heads * rows, width), BF16),
                pltpu.VMEM((heads * rows, latent), F32),
                pltpu.VMEM((heads * rows, 128), F32),
                pltpu.VMEM((8, 64 * rows), F32),
                pltpu.VMEM(q_nope.shape, BF16),
                pltpu.VMEM(q_rope.shape, BF16),
                pltpu.VMEM(w_uk.shape, BF16),
                pltpu.VMEM(w_uv.shape, BF16),
                pltpu.VMEM((cols, heads * vdim), BF16),
                pltpu.VMEM((2, 4, rows, heads * vdim // 2), BF16),
                pltpu.VMEM((4 * rows, 512), BF16),
                pltpu.VMEM((4 * rows, 512), BF16),
                pltpu.VMEM((4, 4, rows, 128), BF16),
                pltpu.VMEM((4, 4, rows, 128), BF16),
                pltpu.VMEM((4, rows, 128), F32),
                pltpu.SemaphoreType.DMA((N_SEMS,)),
                pltpu.SemaphoreType.DMA((N_SEMS,)),
                pltpu.SemaphoreType.DMA((6,)),
            ],
            compiler_params=pltpu.CompilerParams(
                collective_id=0, has_side_effects=True, vmem_limit_bytes=60 * 1024 * 1024
            ),
        )(q_nope, q_rope, kv, w_uk, w_uv, w_out.T, order.reshape(1, groups), mask)

    in_specs = (P("ctx", "tp"), P("ctx", "tp"), P("ctx", None), P("tp", None, None), P("tp", None, None),
                P("tp", "ctx"), P(), P())
    return jax.shard_map(on_device, mesh=mesh, in_specs=in_specs, out_specs=P("ctx", "tp"), check_vma=False)
```

```python
import jax
import jax.numpy as jnp
from jax import lax
from jax.experimental import pallas as pl
from jax.experimental.pallas import tpu as pltpu
from jax.sharding import PartitionSpec as P

MESH = pl.DeviceIdType.MESH
NT = (((1,), (1,)), ((), ()))
NN = (((1,), (0,)), ((), ()))
F32, BF16, I32 = jnp.float32, jnp.bfloat16, jnp.int32
MASKED = -1e30
N_SEMS = 128
SWAP = (1, 2)
RELAY = (0,1,3)


def dot(a, b, dims=NN):
    return lax.dot_general(a, b, dims, preferred_element_type=F32)


def kernel(q_nope_hbm, q_rope_hbm, kv_hbm, w_uk_hbm, w_uv_hbm, w_out_hbm, order, mask, out,
           K, W, Q, acc, lanes, bias, q_nope, q_rope, w_uk, w_uv, w_own, H, XS, XR, S, R, A, send, recv, local):
    heads, nope, latent = w_uk.shape
    rope = q_rope.shape[1] // heads
    half = q_nope.shape[0] // 2
    rows = heads * half
    cols = w_own.shape[0]
    keys = 8 * half
    scale = (nope + rope) ** -0.5 * 1.4426950408889634

    c, t = lax.axis_index("ctx"), lax.axis_index("tp")
    z, x, y = c // 16, (c // 4) % 4, c % 4
    zl, core = t // 2, t % 2
    other = 1 - core

    def dev(dz=0, dx=0, dy=0, dl=0, k=core):
        cc = ((z + dz) % 4) * 16 + ((x + dx) % 4) * 4 + (y + dy) % 4
        return (cc, ((zl + dl) % 4) * 2 + k)

    sibling = dev(k=other)
    barrier = pltpu.get_barrier_semaphore()
    partners = [dev(dz=1), dev(dz=3), dev(dx=1), dev(dx=2), dev(dx=3), sibling]
    partners += [dev(dl=dl, dy=dy) for dl in range(4) for dy in range(4) if dl or dy]
    for p in partners:
        pl.semaphore_signal(barrier, inc=1, device_id=p, device_id_type=MESH)

    own_rows = kv_hbm.at[pl.ds(pl.multiple_of(core * half, half), half)]
    loads = [
        pltpu.make_async_copy(src, dst, local.at[i])
        for i, (src, dst) in enumerate([
            (own_rows, K.at[0, 0, core, 0]), (w_out_hbm, w_own), (q_nope_hbm, q_nope), (q_rope_hbm, q_rope),
            (w_uk_hbm, w_uk), (w_uv_hbm, w_uv)])
    ]
    for d in loads:
        d.start()

    pending, used = [], [0]

    def push(src, dst, to):
        i = used[0]
        used[0] += 1
        d = pltpu.make_async_remote_copy(src, dst, send.at[i], recv.at[i], device_id=to, device_id_type=MESH)
        d.start()
        pending.append(d)
        return d

    done = []

    def sent(d):
        d.wait_send()
        done.append(d)

    def arrived(ds):
        for d in ds:
            d.wait_recv()

    lo, hi = pl.ds(0, half // 2), pl.ds(half // 2, half // 2)

    def first(dz, a):
        return dev(dx=a) if dz not in SWAP else dev(dx=a * other, dy=a * core)

    def second(dz, a):
        return dev(dy=a) if dz not in SWAP else dev(dx=a * core, dy=a * other)

    def kz_send():
        a = K.at[0, 0, core, 0]
        p, q = K.at[3, 0, core, 0], K.at[1, 0, core, 0]
        l1, h2 = push(a.at[lo], p.at[lo], dev(dz=1)), push(a.at[hi], q.at[hi], dev(dz=3))
        h1, l2 = push(a.at[hi], p.at[hi], dev(dz=1)), push(a.at[lo], q.at[lo], dev(dz=3))
        return l1, h2, h1, l2

    def kz_relay():
        return (push(K.at[3, 0, core, 0, lo], K.at[2, 0, core, 0, lo], dev(dz=1)),
                push(K.at[1, 0, core, 0, hi], K.at[2, 0, core, 0, hi], dev(dz=3)))

    def kf_send(dz):
        return [push(K.at[dz, 0, core, 0], K.at[dz, 0, core, 4 - a], first(dz, a)) for a in (2, 1, 3)]

    def kg_send(dz):
        return {4 - a: push(K.at[dz, 0, core], K.at[dz, 4 - a, core], second(dz, a))
                for a in ((1, 3) if dz in RELAY else (1, 3, 2))}

    def kg_relay(dz):
        l, h = pl.ds(0, 2), pl.ds(2, 2)
        return (push(K.at[dz, 3, core, l], K.at[dz, 2, core, l], second(dz, 1)),
                push(K.at[dz, 1, core, h], K.at[dz, 2, core, h], second(dz, 3)))

    def share(dz, s):
        return push(K.at[dz, s, core], K.at[dz, s, core], sibling)

    own_w = W.at[z, x]
    wl, wh = pl.ds(0, 32), pl.ds(32, 32)

    def wz_send(up, down):
        a, b = W.at[z, x, up], W.at[z, x, down]
        return push(a, a, dev(dz=1)), push(b, b, dev(dz=3))

    def wz_relay(at):
        a, b = W.at[(z + 3) % 4, x, pl.ds(at, 16)], W.at[(z + 1) % 4, x, pl.ds(32 + at, 16)]
        return push(a, a, dev(dz=1)), push(b, b, dev(dz=3))

    def wx_send(dz, part, relayed):
        a = W.at[(z + dz) % 4, x, part]
        return [push(a, a, dev(dx=d)) for d in ((1, 3) if relayed else (1, 3, 2))]

    def wx_relay(dz, name):
        d, part = (1, wl) if name == "l" else (3, wh)
        a = W.at[(z + dz) % 4, (x + 4 - d) % 4, part]
        return [push(a, a, dev(dx=d))]

    def attend(dz, s, begin=False):
        kc = K[dz, s].reshape(keys, latent + rope)
        at = (dz * 4 + s) * keys
        for i in range(2):
            r = pl.ds(i * rows, rows)
            p = dot(Q[r, :], kc, NT) * scale + bias[i : i + 1, at : at + keys]
            if begin:
                key = lax.broadcasted_iota(I32, (rows, keys), 1) - i * keys // 2
                row = lax.broadcasted_iota(I32, (rows, keys), 0) % half
                p = jnp.where((key >= 0) & (key < half) & (key > row), MASKED, p)
            w = jnp.exp2(p)
            part = w[:, :128]
            for j in range(128, keys, 128):
                part = part + w[:, j : j + 128]
            added = dot(w.astype(BF16), kc[:, :latent])
            if begin:
                lanes[r, :] = part
                acc[r, :] = added
            else:
                lanes[r, :] += part
                acc[r, :] += added

    groups = order.shape[1]
    named = (lax.broadcasted_iota(I32, (groups, groups), 0) == order[...]).astype(BF16)
    mine = (lax.broadcasted_iota(I32, (8, groups), 1) == 2 * c + lax.broadcasted_iota(I32, (8, groups), 0)).astype(BF16)
    named_mine = dot(mine, named, NT).astype(BF16)
    by_name = dot(named_mine, mask[...].astype(BF16)).astype(BF16)
    by_store = dot(by_name, named).astype(BF16)
    for n in range(16):
        g = lax.broadcasted_iota(I32, (1, keys), 1) // half
        kk, j = g // 4, g % 4
        dz, s = n // 4, n % 4
        dx, dy = (j, s) if dz not in SWAP else (jnp.where(kk == 0, j, s), jnp.where(kk == 0, s, j))
        store = 2 * (((z + dz) % 4) * 16 + ((x + dx) % 4) * 4 + (y + dy) % 4) + kk
        pick = (lax.broadcasted_iota(I32, (groups, keys), 0) == store).astype(BF16)
        bias[:, n * keys : (n + 1) * keys] = (1.0 - dot(by_store, pick)) * MASKED

    loads[1].wait()
    own = jnp.concatenate([w_own[...], jnp.zeros((64 - cols, w_own.shape[1]), BF16)], axis=0)
    W[pl.ds(z, 1), pl.ds(x, 1)] = own[None, None]

    for d in loads[2:5]:
        d.wait()
    for h in range(heads):
        a = dot(q_nope[:, h * nope : (h + 1) * nope], w_uk[h]).astype(BF16)
        b = q_rope[:, h * rope : (h + 1) * rope]
        for i in range(2):
            r = pl.ds(i * rows + h * half, half)
            Q[r, :latent] = a[i * half : (i + 1) * half]
            Q[r, latent:] = b[i * half : (i + 1) * half]

    loads[0].wait()
    pl.semaphore_wait(barrier, len(partners))

    kz = kz_send()
    kf, kg, kg2, sh = {0: kf_send(0)}, {}, {}, {}
    wz = []
    wx, wx2 = {}, {}

    def wx_go(dz, name, relayed=True):
        wx[dz, name] = wx_send(dz, halves[name], relayed)

    def wx_on(dz, name):
        arrived(wx[dz, name])
        wx2[dz, name] = wx_relay(dz, name)

    halves = {"l": wl, "h": wh, "a": pl.ds(0, 16), "b": pl.ds(16, 16), "c": pl.ds(32, 16), "d": pl.ds(48, 16)}
    wx_go(0, "l")
    wx_go(0, "h")

    def pass_on(dz):
        arrived(kf[dz])
        kg[dz] = kg_send(dz)
        sh[dz, 0] = share(dz, 0)

    def hand_over(dz):
        if dz in RELAY:
            arrived([kg[dz][3], kg[dz][1]])
            kg2[dz] = kg_relay(dz)
        for s in (3, 1):
            arrived([] if dz in RELAY else [kg[dz][s]])
            sh[dz, s] = share(dz, s)

    def hand_over_far(dz):
        arrived(kg2[dz] if dz in RELAY else [kg[dz][2]])
        sh[dz, 2] = share(dz, 2)

    def use(dz, s, begin=False):
        arrived([sh[dz, s]])
        attend(dz, s, begin)

    pass_on(0)
    wz.append(wz_send(wl, wh))
    arrived(kz[:2])
    kz2 = kz_relay()
    arrived(kz[2:])
    kf[1], kf[3] = kf_send(1), kf_send(3)
    use(0, 0, True)
    hand_over(0)
    wx_on(0, "l")
    wx_on(0, "h")
    pass_on(1)
    pass_on(3)
    arrived(kz2)
    kf[2] = kf_send(2)
    wz.append(wz_send(wh, wl))
    hand_over_far(0)
    arrived(wz[0])
    wz2 = [wz_relay(0)]
    wx_go(3, "l")
    wx_go(1, "h")
    use(0, 3)
    use(0, 1)
    pass_on(2)
    hand_over(1)
    hand_over(3)
    wz2.append(wz_relay(16))
    use(0, 2)
    arrived(wz[1])
    wx_go(3, "h")
    wx_go(1, "l")
    use(1, 0)
    use(3, 0)
    wx_on(3, "l")
    wx_on(1, "h")
    hand_over_far(1)
    hand_over_far(3)
    use(1, 3)
    use(2, 0)
    use(1, 1)
    hand_over(2)
    arrived(wz2[0])
    wx_go(2, "a", False)
    wx_go(2, "c", False)
    use(3, 3)
    use(3, 1)
    hand_over_far(2)
    use(1, 2)
    wx_on(3, "h")
    wx_on(1, "l")
    use(3, 2)
    use(2, 3)
    arrived(wz2[1])
    wx_go(2, "b", False)
    wx_go(2, "d", False)
    use(2, 1)
    use(2, 2)

    loads[5].wait()
    inv = 1.0 / jnp.sum(lanes[...], axis=1, keepdims=True)
    vdim = w_uv.shape[2]
    piece = heads // 2
    hy = []
    for h in range(heads):
        u, v = h * half, rows + h * half
        a = jnp.concatenate([acc[u : u + half, :] * inv[u : u + half], acc[v : v + half, :] * inv[v : v + half]], axis=0)
        at = (h % piece) * vdim
        H[h // piece, 0, :, at : at + vdim] = dot(a.astype(BF16), w_uv[h]).astype(BF16)
        if h % piece == piece - 1:
            g = h // piece
            hy += [push(H.at[g, 0], H.at[g, 4 - d], dev(dy=d)) for d in (1, 3, 2)]
    for name in "acbd":
        arrived(wx[2, name])
    for d in wx2:
        arrived(wx2[d])
    hy = {(i // 3, (3, 1, 2)[i % 3]): d for i, d in enumerate(hy)}
    arrived([hy[g, d] for g in range(2) for d in (1, 3)])

    deep = W.shape[3] // 2

    def product(k, at):
        w = W[:, pl.ds(2 * k, 2)].reshape(512, 2 * deep)
        a, b = (H[g, at : at + 2].reshape(128, deep) for g in range(2))
        return dot(a, w[:, :deep], NT) + dot(b, w[:, deep:], NT)

    last = []
    for at in (0, 2):
        if at:
            arrived([hy[g, 2] for g in range(2)])
        r = pl.ds(at * 64, 128)
        XS[r, :] = product(other, at).astype(BF16)
        xs = push(XS.at[r], XR.at[r], sibling)
        kept = product(core, at)
        arrived([xs])
        total = (kept + XR[r, :].astype(F32)).astype(BF16)
        for zz in range(4):
            for i in range(2):
                S[zz, at + i] = total[i * 64 : (i + 1) * 64, zz * 128 : (zz + 1) * 128]
        last += [push(S.at[(zl + dl) % 4, dy], R.at[dl, dy], dev(dl=dl, dy=dy))
                 for dl in (2, 3, 1, 0) for dy in (at, at + 1) if dl or dy]
    R[0, 0] = S[pl.ds(zl, 1), 0][0]
    arrived(last)
    for dy in range(4):
        a = R[0, dy].astype(F32) + R[1, dy].astype(F32) + R[2, dy].astype(F32) + R[3, dy].astype(F32)
        A[pl.ds((y + 4 - dy) % 4, 1)] = a[None]
    out[...] = jnp.concatenate(
        [A[yy][:, q * 64 : q * 64 + cols] for q in range(2) for yy in range(4)], axis=1
    ).astype(out.dtype)
    for d in pending:
        if not any(d is e for e in done):
            d.wait_send()


def solution(mesh):
    def on_device(q_nope, q_rope, kv, w_uk, w_uv, w_out, order, mask):
        heads, nope, latent = w_uk.shape
        rows, width = kv.shape
        half, cols = rows // 2, w_out.shape[1]
        vdim = w_uv.shape[2]
        groups = order.shape[0]
        in_vmem = pl.BlockSpec(memory_space=pltpu.VMEM)
        in_hbm = pl.BlockSpec(memory_space=pl.ANY)
        return pl.pallas_call(
            kernel,
            out_shape=jax.ShapeDtypeStruct((rows, 8 * cols), BF16),
            in_specs=[in_hbm] * 6 + [in_vmem] * 2,
            out_specs=in_vmem,
            scratch_shapes=[
                pltpu.VMEM((4, 4, 2, 4, half, width), BF16),
                pltpu.VMEM((4, 4, 64, heads * vdim), BF16),
                pltpu.VMEM((heads * rows, width), BF16),
                pltpu.VMEM((heads * rows, latent), F32),
                pltpu.VMEM((heads * rows, 128), F32),
                pltpu.VMEM((8, 64 * rows), F32),
                pltpu.VMEM(q_nope.shape, BF16),
                pltpu.VMEM(q_rope.shape, BF16),
                pltpu.VMEM(w_uk.shape, BF16),
                pltpu.VMEM(w_uv.shape, BF16),
                pltpu.VMEM((cols, heads * vdim), BF16),
                pltpu.VMEM((2, 4, rows, heads * vdim // 2), BF16),
                pltpu.VMEM((4 * rows, 512), BF16),
                pltpu.VMEM((4 * rows, 512), BF16),
                pltpu.VMEM((4, 4, rows, 128), BF16),
                pltpu.VMEM((4, 4, rows, 128), BF16),
                pltpu.VMEM((4, rows, 128), F32),
                pltpu.SemaphoreType.DMA((N_SEMS,)),
                pltpu.SemaphoreType.DMA((N_SEMS,)),
                pltpu.SemaphoreType.DMA((6,)),
            ],
            compiler_params=pltpu.CompilerParams(
                collective_id=0, has_side_effects=True, vmem_limit_bytes=60 * 1024 * 1024
            ),
        )(q_nope, q_rope, kv, w_uk, w_uv, w_out.T, order.reshape(1, groups), mask)

    in_specs = (P("ctx", "tp"), P("ctx", "tp"), P("ctx", None), P("tp", None, None), P("tp", None, None),
                P("tp", "ctx"), P(), P())
    return jax.shard_map(on_device, mesh=mesh, in_specs=in_specs, out_specs=P("ctx", "tp"), check_vma=False)
```
